512 devices in a mesh: stretch: 64 (over y, x, core), tp: 8 (over z).
Axes of the slice: x: 4, y: 8, z: 8, core: 2. Of those that a mesh axis runs over, the one named last changes fastest.
Arguments:
- queries: bfloat16 [32768, 32, 128], P(('stretch', 'tp')), may hold values from -8 to 8
- keys: bfloat16 [32768, 8, 128], P(('stretch', 'tp')), may hold values from -8 to 8
- values: bfloat16 [32768, 8, 128], P(('stretch', 'tp')), may hold values from -6 to 6
- beacon_queries: bfloat16 [4096, 32, 128], P(('stretch', 'tp')), may hold values from -8 to 8
- beacon_keys: bfloat16 [4096, 8, 128], P(('stretch', 'tp')), may hold values from -8 to 8
- beacon_values: bfloat16 [4096, 8, 128], P(('stretch', 'tp')), may hold values from -6 to 6
- beacon_places: int32 [4096], P('stretch'), may hold values from 0 to 32767, as said below
- visible: int32 [64], P('stretch'), may hold values from 0 to 63, as said below
Outputs:
- token_out: bfloat16 [32768, 32, 128], P(('stretch', 'tp'))
- beacon_out: bfloat16 [4096, 32, 128], P(('stretch', 'tp'))
The draws below stay inside these ranges and needn't reach their ends.
Inputs may be any that keep to these rules, and one draw needn't show every extreme that they name: `beacon_places`: beacon j of stretch c has a position in c * 512 + 8 * j up to c * 512 + 8 * j + 7; the first beacon of a stretch sits at the start of its span and the last at the end of its span. visible[c] is at most c; the last stretch sees all earlier stretches.
All inputs are finite; a program needn't handle non-finite values.
Results may differ from the reference program's by a relative error of at most 0.012.
The reference program's roundings to bfloat16 on the way count: a program that leaves them out, or rounds other values in their place, can miss the bound.
Values may be sent and summed in bfloat16 or wider, within the bound.
No kernel may reach another device: no remote copies, remote signals or barrier semaphores. Data moves between devices by JAX's collectives and lax.ppermute only.
A program may use at most 128 MiB of HBM per device.

```python
import math
import jax
import jax.numpy as jnp
from jax import lax

STRETCH_LEN = 512
RATIO = 8
HEADS = 32
KVH = 8
HD = 128
NB = 64
STRETCHES = 64
TOKENS = 32768
BEACONS = 4096


def base_values(key, shape):
    return jnp.clip(jax.random.normal(key, shape, jnp.float32), -6.0, 6.0)


def asking(key, rows, salt, heads):
    own_key = jax.random.fold_in(key, salt + 40)
    drawn = base_values(own_key, (rows, heads, HD))
    return drawn.astype(jnp.bfloat16)


def answering(key, rows, salt, heads):
    own_key = jax.random.fold_in(key, salt + 50)
    drawn = base_values(own_key, (rows, heads, HD))
    return drawn.astype(jnp.bfloat16)


def draw_queries(key, part):
    return asking(key, TOKENS, 100, HEADS)


def draw_keys(key, part):
    return answering(key, TOKENS, 100, KVH)


def draw_beacon_queries(key, part):
    return asking(key, BEACONS, 200, HEADS)


def draw_beacon_keys(key, part):
    return answering(key, BEACONS, 200, KVH)


def draw_beacon_places(key, part):
    key = jax.random.fold_in(key, 7)
    index = jnp.arange(BEACONS)
    owner = index // NB
    slot = index % NB
    offset = jax.random.randint(key, (BEACONS,), 0, RATIO)
    offset = jnp.where(slot == 0, 0, jnp.where(slot == NB - 1, RATIO - 1, offset))
    return (owner * STRETCH_LEN + RATIO * slot + offset).astype(jnp.int32)


def draw_visible(key, part):
    key = jax.random.fold_in(key, 5)
    stretch_ids = jnp.arange(STRETCHES)
    drawn = jax.random.randint(key, (STRETCHES,), 0, stretch_ids + 1)
    return jnp.where(stretch_ids == STRETCHES - 1, STRETCHES - 1, drawn).astype(jnp.int32)


def levels(stream_key, shape, shards, low, largest):
    factor_of, own = 1.0, jax.random.fold_in(stream_key, 6)
    for dim, blocks in shards:
        steps = jnp.exp(jax.random.uniform(jax.random.fold_in(own, dim), (blocks,), jnp.float32, low / len(shards), largest / len(shards)))
        factor_of = factor_of * jnp.repeat(steps, shape[dim] // blocks).reshape([-1 if axis == dim else 1 for axis in range(len(shape))])
    return factor_of


def normal_values(key, shape, deviation, most, shards=(), kind=jnp.bfloat16):
    factor_of = levels(key, shape, shards, -0.22, 0.18) if shards else 1.0
    values = jax.random.normal(key, shape, jnp.float32) * deviation * factor_of
    return jnp.minimum(jnp.maximum(values, -most), most).astype(kind)


def setup_inputs(seed: int = 0) -> dict:
    seeds = jax.random.split(jax.random.key(seed), 9)
    queries = draw_queries(jax.random.fold_in(seeds[8], 71), 0)
    keys = draw_keys(jax.random.fold_in(seeds[8], 71), 0)
    values = normal_values(seeds[2], (TOKENS, KVH, HD), 1.0, 6.0, ((0, 512),))
    beacon_queries = draw_beacon_queries(jax.random.fold_in(seeds[8], 71), 0)
    beacon_keys = draw_beacon_keys(jax.random.fold_in(seeds[8], 71), 0)
    beacon_values = normal_values(seeds[5], (BEACONS, KVH, HD), 1.0, 6.0, ((0, 512),))
    beacon_places = draw_beacon_places(jax.random.fold_in(seeds[8], 71), 0)
    visible = draw_visible(jax.random.fold_in(seeds[8], 71), 0)
    return dict(queries=queries, keys=keys, values=values, beacon_queries=beacon_queries, beacon_keys=beacon_keys, beacon_values=beacon_values, beacon_places=beacon_places, visible=visible)


ROPE_BASE = 1000000.0


def rotate(vectors, places):
    width = vectors.shape[-1]
    half = width // 2
    steps = jnp.arange(half).astype(jnp.float32)
    freqs = jnp.exp(steps * (-2.0 * math.log(ROPE_BASE) / width))
    angles = places.astype(jnp.float32)[:, None] * freqs[None, :]
    cosine = jnp.concatenate([jnp.cos(angles), jnp.cos(angles)], -1)[:, None, :]
    sine = jnp.concatenate([jnp.sin(angles), jnp.sin(angles)], -1)[:, None, :]
    wide = vectors.astype(jnp.float32)
    turned = jnp.concatenate([-wide[..., half:], wide[..., :half]], -1)
    return (wide * cosine + turned * sine).astype(jnp.bfloat16)


def reference(queries, keys, values, beacon_queries, beacon_keys, beacon_values, beacon_places, visible):
    group = HEADS // KVH
    rows_all = STRETCH_LEN + NB
    scale = HD ** -0.5
    token_places = jnp.arange(TOKENS).astype(jnp.int32)
    q_rot = rotate(queries, token_places)
    k_rot = rotate(keys, token_places)
    bq_rot = rotate(beacon_queries, beacon_places)
    bk_rot = rotate(beacon_keys, beacon_places)
    memory_keys = bk_rot.astype(jnp.float32)
    memory_values = beacon_values.astype(jnp.float32)
    owner = (jnp.arange(BEACONS) // NB).astype(jnp.int32)
    slot = (jnp.arange(BEACONS) % NB).astype(jnp.int32)
    rows = jnp.arange(rows_all).astype(jnp.int32)
    limit = jnp.where(rows < STRETCH_LEN, rows + 1, RATIO * (rows - STRETCH_LEN + 1))
    local_mask = jnp.arange(STRETCH_LEN)[None, :] < limit[:, None]

    def one_stretch(stretch_id):
        start = (stretch_id * STRETCH_LEN).astype(jnp.int32)
        bstart = (stretch_id * NB).astype(jnp.int32)
        qs = lax.dynamic_slice_in_dim(q_rot, start, STRETCH_LEN, 0)
        bqs = lax.dynamic_slice_in_dim(bq_rot, bstart, NB, 0)
        ks = lax.dynamic_slice_in_dim(k_rot, start, STRETCH_LEN, 0).astype(jnp.float32)
        vs = lax.dynamic_slice_in_dim(values, start, STRETCH_LEN, 0).astype(jnp.float32)
        asked = jnp.concatenate([qs, bqs], 0).astype(jnp.float32).reshape(rows_all, KVH, group, HD)
        near = jnp.einsum('rkgd,skd->kgrs', asked, ks) * scale
        near = jnp.where(local_mask, near, -jnp.inf)
        reach = visible[stretch_id]
        earlier = (owner < stretch_id) & (owner >= stretch_id - reach)
        own = (owner == stretch_id)[None, :] & (rows[:, None] >= STRETCH_LEN) & (slot[None, :] <= rows[:, None] - STRETCH_LEN)
        allowed = earlier[None, :] | own
        far = jnp.einsum('rkgd,skd->kgrs', asked, memory_keys) * scale
        far = jnp.where(allowed, far, -jnp.inf)
        joined = jnp.concatenate([near, far], -1)
        top = jnp.max(joined, -1)
        weights = jnp.exp(joined - top[..., None])
        total = jnp.sum(weights, -1)
        rounded = lax.optimization_barrier(weights.astype(jnp.bfloat16)).astype(jnp.float32)
        summed = jnp.einsum('kgrs,skd->kgrd', rounded[..., :STRETCH_LEN], vs)
        summed = summed + jnp.einsum('kgrs,skd->kgrd', rounded[..., STRETCH_LEN:], memory_values)
        result = (summed / total[..., None]).transpose(2, 0, 1, 3).reshape(rows_all, HEADS, HD).astype(jnp.bfloat16)
        return result[:STRETCH_LEN], result[STRETCH_LEN:]

    raw, beacon = lax.map(one_stretch, jnp.arange(STRETCHES).astype(jnp.int32))
    return raw.reshape(TOKENS, HEADS, HD), beacon.reshape(BEACONS, HEADS, HD)
```

```python
import math, functools
import jax, jax.numpy as jnp
from jax import lax
from jax.experimental import pallas as pl
from jax.experimental.pallas import tpu as pltpu
BIG = -1e30
C2 = 128 ** -0.5 * math.log2(math.e)

def attend(info, x, pieces, tsub=4, chunk=1024, near_static=True):
    np_ = len(pieces)
    S, R = x.shape[0], x.shape[1]
    QR = 288; NT = 64
    per = chunk // 64
    rows = QR
    def dotqk(a, b):
        return lax.dot_general(a, b, (((1,), (1,)), ((), ())), preferred_element_type=jnp.float32)
    def dotpv(a, b):
        return jnp.dot(a, b, preferred_element_type=jnp.float32)
    def kernel(info_ref, x_ref, *rest):
        p_refs = rest[:np_]
        o_ref = rest[np_]
        q2, kk, vv, m_s, acc_s = rest[np_ + 1:]
        me = info_ref[0]; own_y = info_ref[1]; reach = info_ref[2]
        ones = jnp.ones((64, 128), jnp.bfloat16)
        for s in range(S):
            k = x_ref[s, 288:352, :]
            kk[pl.ds(s * 64, 64), :128] = k
            kk[pl.ds(s * 64, 64), 128:] = k
            vv[pl.ds(s * 64, 64), :128] = x_ref[s, 352:416, :]
            vv[pl.ds(s * 64, 64), 128:] = ones
            qs = x_ref[s, 0:288, :].astype(jnp.float32) * C2
            hi = qs.astype(jnp.bfloat16)
            q2[s, :, :128] = hi
            q2[s, :, 128:] = (qs - hi.astype(jnp.float32)).astype(jnp.bfloat16)
        b = p_refs[0][own_y]
        kk[pl.ds(512, 64), :128] = b[:, :128]
        kk[pl.ds(512, 64), 128:] = b[:, :128]
        vv[pl.ds(512, 64), :128] = b[:, 128:]
        vv[pl.ds(512, 64), 128:] = ones
        n = jnp.int32(0)
        for p in range(np_):
            for y in range(8):
                owner = y * 8 + info_ref[3 + p]
                seen = (owner < me) & (owner >= me - reach)
                @pl.when(seen)
                def _():
                    at = pl.ds(pl.multiple_of(576 + n * 64, 64), 64)
                    b = p_refs[p][y]
                    kk[at, :128] = b[:, :128]
                    kk[at, 128:] = b[:, :128]
                    vv[at, :128] = b[:, 128:]
                    vv[at, 128:] = ones
                n = n + seen.astype(jnp.int32)
        full = n // per
        left = n - full * per
        @pl.when(left > 0)
        def _():
            for j in range(1, per):
                @pl.when(j >= left)
                def _():
                    at = pl.ds(pl.multiple_of(576 + (full * per + j) * 64, 64), 64)
                    kk[at, :] = jnp.zeros((64, 256), jnp.bfloat16)
                    vv[at, :] = jnp.zeros((64, 256), jnp.bfloat16)
        def fold(s, sc, v):
            top = m_s[s]
            new = jnp.maximum(top, jnp.max(sc, -1, keepdims=True))
            w = jnp.exp2(sc - new[:, :1])
            fade = jnp.exp2(top - new)
            m_s[s] = new
            f2 = jnp.concatenate([fade, fade], -1)
            acc_s[s] = acc_s[s] * f2 + dotpv(w.astype(jnp.bfloat16), v)
        for s in range(S):
            kw = -(-(s + 1) * 64 // 128) * 128
            sc = dotqk(q2[s], kk[0:kw, :])
            r = lax.broadcasted_iota(jnp.int32, (QR, 1), 0)
            lim = jnp.where(r < 256, s * 64 + r // 4 + 1, s * 64 + ((r - 256) // 4 + 1) * 8)
            col = lax.broadcasted_iota(jnp.int32, (QR, kw), 1)
            sc = jnp.where(col < lim, sc, BIG)
            new = jnp.max(sc, -1, keepdims=True)
            w = jnp.exp2(sc - new).astype(jnp.bfloat16)
            m_s[s] = jnp.broadcast_to(new, (QR, 128))
            acc_s[s] = dotpv(w, vv[0:kw, :])
            sb = dotqk(q2[s, 256:, :], kk[512:576, :])
            rb = lax.broadcasted_iota(jnp.int32, (32, 1), 0) // 4 + s * 8
            cb = lax.broadcasted_iota(jnp.int32, (32, 64), 1)
            sb = jnp.where(cb <= rb, sb, BIG)
            top = m_s[s, 256:, :]
            new = jnp.maximum(top, jnp.max(sb, -1, keepdims=True))
            w = jnp.exp2(sb - new[:, :1]).astype(jnp.bfloat16)
            fade = jnp.exp2(top - new)
            m_s[s, 256:, :] = new
            acc_s[s, 256:, :] = acc_s[s, 256:, :] * jnp.concatenate([fade, fade], -1) + dotpv(w, vv[512:576, :])
        def far(i, _):
            at = pl.ds(pl.multiple_of(576 + i * chunk, 64), chunk)
            k = kk[at, :]; v = vv[at, :]
            def group(g, _):
                for t in range(tsub):
                    s = g * tsub + t
                    fold(s, dotqk(q2[s], k), v)
                return 0
            lax.fori_loop(0, S // tsub, group, 0)
            return 0
        lax.fori_loop(0, full, far, 0)
        @pl.when(left > 0)
        def _():
            at = pl.ds(pl.multiple_of(576 + full * chunk, 64), chunk)
            k = kk[at, :]; v = vv[at, :]
            col = lax.broadcasted_iota(jnp.int32, (QR, chunk), 1)
            def group(g, _):
                for t in range(tsub):
                    s = g * tsub + t
                    sc = jnp.where(col < left * 64, dotqk(q2[s], k), BIG)
                    fold(s, sc, v)
                return 0
            lax.fori_loop(0, S // tsub, group, 0)
        for s in range(S):
            a = acc_s[s]
            o_ref[s] = (a[:, :128] / a[:, 128:]).astype(jnp.bfloat16)
    vm = pl.BlockSpec(memory_space=pltpu.VMEM)
    return pl.pallas_call(
        kernel,
        out_shape=jax.ShapeDtypeStruct((S, QR, 128), jnp.bfloat16),
        in_specs=[pl.BlockSpec(memory_space=pltpu.SMEM)] + [vm] * (1 + np_),
        out_specs=vm,
        scratch_shapes=[
            pltpu.VMEM((S, QR, 256), jnp.bfloat16),
            pltpu.VMEM((576 + 4096 + chunk, 256), jnp.bfloat16),
            pltpu.VMEM((576 + 4096 + chunk, 256), jnp.bfloat16),
            pltpu.VMEM((S, QR, 128), jnp.float32),
            pltpu.VMEM((S, QR, 256), jnp.float32),
        ],
        compiler_params=pltpu.CompilerParams(vmem_limit_bytes=48 * 1024 * 1024),
        name="attend",
    )(info, x, *pieces)


from jax.sharding import Mesh, PartitionSpec as P
ROPE_BASE = 1000000.0


def turns(places, width):
    half = width // 2
    steps = jnp.arange(half).astype(jnp.float32)
    freqs = jnp.exp(steps * (-2.0 * math.log(ROPE_BASE) / width))
    angles = places.astype(jnp.float32)[:, None] * freqs[None, :]
    cosine, sine = jnp.cos(angles), jnp.sin(angles)
    return (
        jnp.concatenate([cosine, cosine], -1)[:, None, :],
        jnp.concatenate([-sine, sine], -1)[:, None, :],
    )


def rotate(vectors, cosine, sine):
    half = vectors.shape[-1] // 2
    wide = vectors.astype(jnp.float32)
    turned = jnp.concatenate([wide[..., half:], wide[..., :half]], -1)
    return (wide * cosine + turned * sine).astype(jnp.bfloat16)


def shift(value, axis, size, step):
    return lax.ppermute(value, axis, [(i, (i + step) % size) for i in range(size)])


def shards(sizes, queries, keys, values, bq, bk, bv, places, visible):
    ny, nx, nc, nt = sizes
    y, x, c, t = (lax.axis_index(a) for a in ("y", "x", "core", "tp"))
    me = (y * nx + x) * nc + c
    span, heads, width = queries.shape
    count = bk.shape[0]
    kvh = bk.shape[1]
    group = heads // kvh
    mine = lax.dynamic_slice_in_dim(places, t * count, count, 0)
    bturn = turns(mine, width)
    memory = jnp.concatenate([rotate(bk, *bturn), bv], -1).transpose(1, 0, 2)
    memory = jnp.broadcast_to(memory[None], (ny, kvh, count, 2 * width))
    memory = memory.reshape(ny * kvh, count, 2 * width)
    own = lax.all_to_all(memory, ("y", "tp"), 0, 0, tiled=True)
    own = own.reshape(ny, nt * count, 2 * width)
    steps = (1, nx - 1, 2)
    pieces = [own] + [shift(own, "x", nx, d) for d in steps]
    pieces = pieces + [shift(p, "core", nc, 1) for p in pieces]
    column = [lax.rem(x + nx - d, nx) for d in (0,) + steps]
    labels = [a * nc + c for a in column] + [a * nc + 1 - c for a in column]
    info = jnp.stack([me, y, visible[0]] + labels).astype(jnp.int32)

    turn = turns(me * span * nt + t * span + jnp.arange(span), width)

    def split(value):
        value = value.reshape(value.shape[0], kvh, -1, width).transpose(1, 0, 2, 3)
        return value.reshape(kvh, -1, width)

    packed = jnp.concatenate(
        [split(rotate(queries, *turn)), split(rotate(bq, *bturn)), split(rotate(keys, *turn)), split(values)], 1
    )
    packed = lax.all_to_all(packed, "tp", 0, 0, tiled=True)
    result = attend(info, packed, pieces)
    result = lax.all_to_all(result, "tp", 0, 0, tiled=True)

    def join(value):
        value = value.reshape(kvh, -1, group, width).transpose(1, 0, 2, 3)
        return value.reshape(-1, heads, width)

    return join(result[:, : span * group]), join(result[:, span * group :])


def solution(mesh):
    sizes = (8, 4, 2, 8)
    names = ("y", "x", "core", "tp")
    grid = Mesh(mesh.devices.reshape(sizes), names)
    rows = P(names, None, None)
    along = P(names[:3])
    return jax.shard_map(
        functools.partial(shards, sizes),
        mesh=grid,
        in_specs=(rows,) * 6 + (along, along),
        out_specs=(rows, rows),
        check_vma=False,
    )
```

```python
import functools
import math

import jax
import jax.numpy as jnp
from jax import lax
from jax.experimental import pallas as pl
from jax.experimental.pallas import tpu as pltpu

BIG = -1e30
LIMIT = 2.0**100
SCALE = 128**-0.5 * math.log2(math.e)


def attend(info, packed, pieces, chunk=2048, block=768, ahead=1):
    sources = packed.shape[0]
    asked, width, near = 288, 128, 512
    rows = sources * asked
    blocks = rows // block
    beacons = len(pieces) * 8 * 64
    per = chunk // 64
    slow = 512

    def scores(k, q):
        return lax.dot_general(k, q, (((1,), (1,)), ((), ())), preferred_element_type=jnp.float32)

    def kernel(info_ref, packed_ref, *rest):
        piece_refs, out_ref = rest[: len(pieces)], rest[len(pieces)]
        q2, local, far, top, total, extra = rest[len(pieces) + 1 :]
        me, own_y, reach = info_ref[0], info_ref[1], info_ref[2]
        for s in range(sources):
            at = pl.ds(s * 64, 64)
            local[at, :width] = packed_ref[s, 288:352, :]
            local[at, width:] = packed_ref[s, 352:416, :]
            scaled = packed_ref[s, 0:asked, :].astype(jnp.float32) * SCALE
            high = scaled.astype(jnp.bfloat16)
            q2[pl.ds(s * asked, asked), :width] = high
            q2[pl.ds(s * asked, asked), width:] = (scaled - high.astype(jnp.float32)).astype(jnp.bfloat16)
        local[pl.ds(near, 64), :] = piece_refs[0][own_y]
        local[pl.ds(near + 64, 64), :] = jnp.zeros((64, 2 * width), jnp.bfloat16)
        count = jnp.int32(0)
        for p in range(len(pieces)):
            for y in range(8):
                owner = y * 8 + info_ref[3 + p]
                seen = (owner < me) & (owner >= me - reach)
                slot = jnp.where(seen, count, 63 - (p * 8 + y - count))
                far[pl.ds(pl.multiple_of(slot * 64, 64), 64), :] = piece_refs[p][y]
                count = count + seen.astype(jnp.int32)

        def double(kv):
            return jnp.concatenate([kv[:, :width], kv[:, :width]], -1)

        def turned(kv):
            v = kv[:, width:]
            return jnp.concatenate([v.T, jnp.ones((16, v.shape[0]), jnp.bfloat16)], 0)

        def query(r):
            return q2[pl.ds(pl.multiple_of(r * block, block), block), :]

        beacon_kv = local[near : near + 128, :]
        beacon_k = double(beacon_kv)
        local_k = double(local[:near, :])
        local_v = turned(local[:near, :])
        beacon_v = turned(beacon_kv)
        for r in range(blocks):
            last = ((r + 1) * block - 1) // asked
            wide = -(-(last + 1) * 64 // 128) * 128
            st = scores(local_k[:wide], query(r))
            sb = scores(beacon_k, query(r))
            row = lax.broadcasted_iota(jnp.int32, (1, block), 1) + r * block
            s = row // asked
            u = row - s * asked
            token = u < 256
            until = jnp.where(token, s * 64 + u // 4 + 1, s * 64 + ((u - 256) // 4 + 1) * 8)
            until_b = jnp.where(token, 0, s * 8 + (u - 256) // 4 + 1)
            st = jnp.where(lax.broadcasted_iota(jnp.int32, (wide, block), 0) < until, st, BIG)
            sb = jnp.where(lax.broadcasted_iota(jnp.int32, (128, block), 0) < until_b, sb, BIG)
            m = jnp.maximum(jnp.max(st, 0, keepdims=True), jnp.max(sb, 0, keepdims=True))
            top[r] = m
            total[r] = jnp.dot(
                local_v[:, :wide], jnp.exp2(st - m).astype(jnp.bfloat16), preferred_element_type=jnp.float32
            ) + jnp.dot(beacon_v, jnp.exp2(sb - m).astype(jnp.bfloat16), preferred_element_type=jnp.float32)

        extra[...] = jnp.zeros_like(extra)
        full = count // per
        left = count - full * per

        def sweep(start, keys):
            kv = far[pl.ds(pl.multiple_of(start, 64), chunk), :]
            k, v = double(kv), turned(kv)
            if keys is not None:
                v = jnp.where(lax.broadcasted_iota(jnp.int32, v.shape, 1) < keys, v, jnp.zeros_like(v))
            waiting = []

            def finish(r, st):
                w = jnp.exp2(st - top[r]).astype(jnp.bfloat16)
                extra[r] += jnp.dot(v, w, preferred_element_type=jnp.float32)

            for r in range(blocks):
                waiting.append((r, scores(k, query(r))))
                if len(waiting) > ahead:
                    finish(*waiting.pop(0))
            for item in waiting:
                finish(*item)

        def step(i, _):
            sweep(i * chunk, None)
            return 0

        lax.fori_loop(0, full, step, 0)

        @pl.when(left > 0)
        def _():
            sweep(full * chunk, left * 64)

        worst = jnp.max(jnp.where(extra[:, width : width + 8, :] <= LIMIT, 0.0, 1.0))

        @pl.when(worst > 0.0)
        def _():
            extra[...] = jnp.zeros_like(extra)

            def redo(i, _):
                start = pl.multiple_of(i * slow, 64)
                kv = far[pl.ds(start, slow), :]
                k, v = double(kv), turned(kv)
                inside = lax.broadcasted_iota(jnp.int32, (slow, block), 0) < count * 64 - start

                def one(r, _):
                    st = jnp.where(inside, scores(k, query(r)), BIG)
                    old = top[r]
                    m = jnp.maximum(old, jnp.max(st, 0, keepdims=True))
                    w = jnp.exp2(st - m).astype(jnp.bfloat16)
                    top[r] = m
                    total[r] = total[r] * jnp.exp2(old - m) + jnp.dot(v, w, preferred_element_type=jnp.float32)
                    return 0

                lax.fori_loop(0, blocks, one, 0)
                return 0

            lax.fori_loop(0, (count + slow // 64 - 1) // (slow // 64), redo, 0)

        parts = []
        for r in range(blocks):
            a = total[r] + extra[r]
            parts.append((a[:width] / a[width : width + 1]).T.astype(jnp.bfloat16))
        joined = jnp.concatenate(parts, 0)
        for s in range(sources):
            out_ref[s] = joined[s * asked : (s + 1) * asked]

    vmem = pl.BlockSpec(memory_space=pltpu.VMEM)
    return pl.pallas_call(
        kernel,
        out_shape=jax.ShapeDtypeStruct((sources, asked, width), jnp.bfloat16),
        in_specs=[pl.BlockSpec(memory_space=pltpu.SMEM)] + [vmem] * (1 + len(pieces)),
        out_specs=vmem,
        scratch_shapes=[
            pltpu.VMEM((rows, 2 * width), jnp.bfloat16),
            pltpu.VMEM((near + 128, 2 * width), jnp.bfloat16),
            pltpu.VMEM((beacons, 2 * width), jnp.bfloat16),
            pltpu.VMEM((blocks, 1, block), jnp.float32),
            pltpu.VMEM((blocks, width + 16, block), jnp.float32),
            pltpu.VMEM((blocks, width + 16, block), jnp.float32),
        ],
        compiler_params=pltpu.CompilerParams(vmem_limit_bytes=48 * 1024 * 1024),
        name="attend",
    )(info, packed, *pieces)


from jax.sharding import Mesh, PartitionSpec as P
ROPE_BASE = 1000000.0


def turns(places, width):
    half = width // 2
    steps = jnp.arange(half).astype(jnp.float32)
    freqs = jnp.exp(steps * (-2.0 * math.log(ROPE_BASE) / width))
    angles = places.astype(jnp.float32)[:, None] * freqs[None, :]
    cosine, sine = jnp.cos(angles), jnp.sin(angles)
    return (
        jnp.concatenate([cosine, cosine], -1)[:, None, :],
        jnp.concatenate([-sine, sine], -1)[:, None, :],
    )


def rotate(vectors, cosine, sine):
    half = vectors.shape[-1] // 2
    wide = vectors.astype(jnp.float32)
    turned = jnp.concatenate([wide[..., half:], wide[..., :half]], -1)
    return (wide * cosine + turned * sine).astype(jnp.bfloat16)


def shift(value, axis, size, step):
    return lax.ppermute(value, axis, [(i, (i + step) % size) for i in range(size)])


def shards(sizes, queries, keys, values, bq, bk, bv, places, visible):
    ny, nx, nc, nt = sizes
    y, x, c, t = (lax.axis_index(a) for a in ("y", "x", "core", "tp"))
    me = (y * nx + x) * nc + c
    span, heads, width = queries.shape
    count = bk.shape[0]
    kvh = bk.shape[1]
    group = heads // kvh
    mine = lax.dynamic_slice_in_dim(places, t * count, count, 0)
    bturn = turns(mine, width)
    memory = jnp.concatenate([rotate(bk, *bturn), bv], -1).transpose(1, 0, 2)
    memory = jnp.broadcast_to(memory[None], (ny, kvh, count, 2 * width))
    memory = memory.reshape(ny * kvh, count, 2 * width)
    own = lax.all_to_all(memory, ("y", "tp"), 0, 0, tiled=True)
    own = own.reshape(ny, nt * count, 2 * width)
    steps = (1, nx - 1, 2)
    pieces = [own] + [shift(own, "x", nx, d) for d in steps]
    pieces = pieces + [shift(p, "core", nc, 1) for p in pieces]
    column = [lax.rem(x + nx - d, nx) for d in (0,) + steps]
    labels = [a * nc + c for a in column] + [a * nc + 1 - c for a in column]
    info = jnp.stack([me, y, visible[0]] + labels).astype(jnp.int32)

    turn = turns(me * span * nt + t * span + jnp.arange(span), width)

    def split(value):
        value = value.reshape(value.shape[0], kvh, -1, width).transpose(1, 0, 2, 3)
        return value.reshape(kvh, -1, width)

    packed = jnp.concatenate(
        [split(rotate(queries, *turn)), split(rotate(bq, *bturn)), split(rotate(keys, *turn)), split(values)], 1
    )
    packed = lax.all_to_all(packed, "tp", 0, 0, tiled=True)
    result = attend(info, packed, pieces)
    result = lax.all_to_all(result, "tp", 0, 0, tiled=True)

    def join(value):
        value = value.reshape(kvh, -1, group, width).transpose(1, 0, 2, 3)
        return value.reshape(-1, heads, width)

    return join(result[:, : span * group]), join(result[:, span * group :])


def solution(mesh):
    sizes = (8, 4, 2, 8)
    names = ("y", "x", "core", "tp")
    grid = Mesh(mesh.devices.reshape(sizes), names)
    rows = P(names, None, None)
    along = P(names[:3])
    return jax.shard_map(
        functools.partial(shards, sizes),
        mesh=grid,
        in_specs=(rows,) * 6 + (along, along),
        out_specs=(rows, rows),
        check_vma=False,
    )
```

```python
import functools
import math

import jax
import jax.numpy as jnp
from jax import lax
from jax.experimental import pallas as pl
from jax.experimental.pallas import tpu as pltpu
from jax.sharding import Mesh
from jax.sharding import PartitionSpec as P

BIG = -1e30
LIMIT = 2.0**100
SCALE = 128**-0.5 * math.log2(math.e)


def attend(info, packed, pieces, chunk=2048, block=768, ahead=1):
    sources = packed.shape[0]
    asked, width, near = 288, 128, 512
    rows = sources * asked
    blocks = rows // block
    beacons = len(pieces) * 8 * 64
    per = chunk // 64
    slow = 512

    def scores(k, q):
        return lax.dot_general(k, q, (((1,), (1,)), ((), ())), preferred_element_type=jnp.float32)

    def kernel(info_ref, packed_ref, *rest):
        piece_refs, out_ref = rest[: len(pieces)], rest[len(pieces)]
        q2, local, far, top, total, extra = rest[len(pieces) + 1 :]
        me, own_y, reach = info_ref[0], info_ref[1], info_ref[2]
        for s in range(sources):
            at = pl.ds(s * 64, 64)
            local[at, :width] = packed_ref[s, 288:352, :]
            local[at, width:] = packed_ref[s, 352:416, :]
            scaled = packed_ref[s, 0:asked, :].astype(jnp.float32) * SCALE
            high = scaled.astype(jnp.bfloat16)
            q2[pl.ds(s * asked, asked), :width] = high
            q2[pl.ds(s * asked, asked), width:] = (scaled - high.astype(jnp.float32)).astype(jnp.bfloat16)
        local[pl.ds(near, 64), :] = piece_refs[0][own_y]
        local[pl.ds(near + 64, 64), :] = jnp.zeros((64, 2 * width), jnp.bfloat16)
        count = jnp.int32(0)
        for p in range(len(pieces)):
            for y in range(8):
                owner = y * 8 + info_ref[3 + p]
                seen = (owner < me) & (owner >= me - reach)
                slot = jnp.where(seen, count, 63 - (p * 8 + y - count))
                far[pl.ds(pl.multiple_of(slot * 64, 64), 64), :] = piece_refs[p][y]
                count = count + seen.astype(jnp.int32)

        def double(kv):
            return jnp.concatenate([kv[:, :width], kv[:, :width]], -1)

        def turned(kv):
            v = kv[:, width:]
            return jnp.concatenate([v.T, jnp.ones((16, v.shape[0]), jnp.bfloat16)], 0)

        def query(r):
            return q2[pl.ds(pl.multiple_of(r * block, block), block), :]

        beacon_kv = local[near : near + 128, :]
        beacon_k = double(beacon_kv)
        local_k = double(local[:near, :])
        local_v = turned(local[:near, :])
        beacon_v = turned(beacon_kv)
        for r in range(blocks):
            last = ((r + 1) * block - 1) // asked
            wide = -(-(last + 1) * 64 // 128) * 128
            st = scores(local_k[:wide], query(r))
            sb = scores(beacon_k, query(r))
            row = lax.broadcasted_iota(jnp.int32, (1, block), 1) + r * block
            s = row // asked
            u = row - s * asked
            token = u < 256
            until = jnp.where(token, s * 64 + u // 4 + 1, s * 64 + ((u - 256) // 4 + 1) * 8)
            until_b = jnp.where(token, 0, s * 8 + (u - 256) // 4 + 1)
            st = jnp.where(lax.broadcasted_iota(jnp.int32, (wide, block), 0) < until, st, BIG)
            sb = jnp.where(lax.broadcasted_iota(jnp.int32, (128, block), 0) < until_b, sb, BIG)
            m = jnp.maximum(jnp.max(st, 0, keepdims=True), jnp.max(sb, 0, keepdims=True))
            top[r] = m
            total[r] = jnp.dot(
                local_v[:, :wide], jnp.exp2(st - m).astype(jnp.bfloat16), preferred_element_type=jnp.float32
            ) + jnp.dot(beacon_v, jnp.exp2(sb - m).astype(jnp.bfloat16), preferred_element_type=jnp.float32)

        extra[...] = jnp.zeros_like(extra)
        full = count // per
        left = count - full * per

        def sweep(start, keys):
            kv = far[pl.ds(pl.multiple_of(start, 64), chunk), :]
            k, v = double(kv), turned(kv)
            if keys is not None:
                v = jnp.where(lax.broadcasted_iota(jnp.int32, v.shape, 1) < keys, v, jnp.zeros_like(v))
            waiting = []

            def finish(r, st):
                w = jnp.exp2(st - top[r]).astype(jnp.bfloat16)
                extra[r] += jnp.dot(v, w, preferred_element_type=jnp.float32)

            for r in range(blocks):
                waiting.append((r, scores(k, query(r))))
                if len(waiting) > ahead:
                    finish(*waiting.pop(0))
            for item in waiting:
                finish(*item)

        def step(i, _):
            sweep(i * chunk, None)
            return 0

        lax.fori_loop(0, full, step, 0)

        @pl.when(left > 0)
        def _():
            sweep(full * chunk, left * 64)

        worst = jnp.max(jnp.where(extra[:, width : width + 8, :] <= LIMIT, 0.0, 1.0))

        @pl.when(worst > 0.0)
        def _():
            extra[...] = jnp.zeros_like(extra)

            def redo(i, _):
                start = pl.multiple_of(i * slow, 64)
                kv = far[pl.ds(start, slow), :]
                k, v = double(kv), turned(kv)
                inside = lax.broadcasted_iota(jnp.int32, (slow, block), 0) < count * 64 - start

                def one(r, _):
                    st = jnp.where(inside, scores(k, query(r)), BIG)
                    old = top[r]
                    m = jnp.maximum(old, jnp.max(st, 0, keepdims=True))
                    w = jnp.exp2(st - m).astype(jnp.bfloat16)
                    top[r] = m
                    total[r] = total[r] * jnp.exp2(old - m) + jnp.dot(v, w, preferred_element_type=jnp.float32)
                    return 0

                lax.fori_loop(0, blocks, one, 0)
                return 0

            lax.fori_loop(0, (count + slow // 64 - 1) // (slow // 64), redo, 0)

        parts = []
        for r in range(blocks):
            a = total[r] + extra[r]
            parts.append((a[:width] / a[width : width + 1]).T.astype(jnp.bfloat16))
        joined = jnp.concatenate(parts, 0)
        for s in range(sources):
            out_ref[s] = joined[s * asked : (s + 1) * asked]

    vmem = pl.BlockSpec(memory_space=pltpu.VMEM)
    return pl.pallas_call(
        kernel,
        out_shape=jax.ShapeDtypeStruct((sources, asked, width), jnp.bfloat16),
        in_specs=[pl.BlockSpec(memory_space=pltpu.SMEM)] + [vmem] * (1 + len(pieces)),
        out_specs=vmem,
        scratch_shapes=[
            pltpu.VMEM((rows, 2 * width), jnp.bfloat16),
            pltpu.VMEM((near + 128, 2 * width), jnp.bfloat16),
            pltpu.VMEM((beacons, 2 * width), jnp.bfloat16),
            pltpu.VMEM((blocks, 1, block), jnp.float32),
            pltpu.VMEM((blocks, width + 16, block), jnp.float32),
            pltpu.VMEM((blocks, width + 16, block), jnp.float32),
        ],
        compiler_params=pltpu.CompilerParams(vmem_limit_bytes=48 * 1024 * 1024),
        name="attend",
    )(info, packed, *pieces)


def memory_rows(t, places, bk, bv, copies):
    count, kvh, width = bk.shape
    half = width // 2

    def kernel(t_ref, places_ref, bk_ref, bv_ref, out_ref):
        row = lax.broadcasted_iota(jnp.int32, (count, width), 0)
        place = jnp.zeros((count, width), jnp.int32)
        for j in range(count):
            place = jnp.where(row == j, places_ref[t_ref[0] * count + j], place)
        steps = (lax.broadcasted_iota(jnp.int32, (count, width), 1) % half).astype(jnp.float32)
        angles = place.astype(jnp.float32) * jnp.exp(steps * (-2.0 * math.log(ROPE_BASE) / width))
        cosine, sine = jnp.cos(angles), jnp.sin(angles)
        sine = jnp.where(lax.broadcasted_iota(jnp.int32, (count, width), 1) < half, -sine, sine)
        wide = bk_ref[...].astype(jnp.float32)
        keys, vals = [], bv_ref[...].astype(jnp.float32)
        for h in range(kvh):
            k = wide[:, h, :]
            k = k * cosine + pltpu.roll(k, half, 1) * sine
            both = jnp.concatenate([k, vals[:, h, :]], -1).astype(jnp.bfloat16)
            for y in range(copies):
                out_ref[y * kvh + h] = both

    vmem = pl.BlockSpec(memory_space=pltpu.VMEM)
    smem = pl.BlockSpec(memory_space=pltpu.SMEM)
    return pl.pallas_call(
        kernel,
        out_shape=jax.ShapeDtypeStruct((copies * kvh, count, 2 * width), jnp.bfloat16),
        in_specs=[smem, smem, vmem, vmem],
        out_specs=vmem,
        name="memory_rows",
    )(t, places, bk, bv)


ROPE_BASE = 1000000.0


def turns(places, width):
    half = width // 2
    steps = jnp.arange(half).astype(jnp.float32)
    freqs = jnp.exp(steps * (-2.0 * math.log(ROPE_BASE) / width))
    angles = places.astype(jnp.float32)[:, None] * freqs[None, :]
    cosine, sine = jnp.cos(angles), jnp.sin(angles)
    return (
        jnp.concatenate([cosine, cosine], -1)[:, None, :],
        jnp.concatenate([-sine, sine], -1)[:, None, :],
    )


def rotate(vectors, cosine, sine):
    half = vectors.shape[-1] // 2
    wide = vectors.astype(jnp.float32)
    turned = jnp.concatenate([wide[..., half:], wide[..., :half]], -1)
    return (wide * cosine + turned * sine).astype(jnp.bfloat16)


def shift(value, axis, size, step):
    return lax.ppermute(value, axis, [(i, (i + step) % size) for i in range(size)])


def shards(sizes, queries, keys, values, bq, bk, bv, places, visible):
    ny, nx, nc, nt = sizes
    y, x, c, t = (lax.axis_index(a) for a in ("y", "x", "core", "tp"))
    me = (y * nx + x) * nc + c
    span, heads, width = queries.shape
    count = bk.shape[0]
    kvh = bk.shape[1]
    group = heads // kvh
    mine = lax.dynamic_slice_in_dim(places, t * count, count, 0)
    bturn = turns(mine, width)
    memory = memory_rows(t.reshape(1), places, bk, bv, ny)
    own = lax.all_to_all(memory, ("y", "tp"), 0, 0, tiled=True)
    own = own.reshape(ny, nt * count, 2 * width)
    steps = (1, nx - 1, 2)
    pieces = [own] + [shift(own, "x", nx, d) for d in steps]
    pieces = pieces + [shift(p, "core", nc, 1) for p in pieces]
    column = [lax.rem(x + nx - d, nx) for d in (0,) + steps]
    labels = [a * nc + c for a in column] + [a * nc + 1 - c for a in column]
    info = jnp.stack([me, y, visible[0]] + labels).astype(jnp.int32)

    turn = turns(me * span * nt + t * span + jnp.arange(span), width)

    def split(value):
        value = value.reshape(value.shape[0], kvh, -1, width).transpose(1, 0, 2, 3)
        return value.reshape(kvh, -1, width)

    packed = jnp.concatenate(
        [split(rotate(queries, *turn)), split(rotate(bq, *bturn)), split(rotate(keys, *turn)), split(values)], 1
    )
    packed = lax.all_to_all(packed, "tp", 0, 0, tiled=True)
    result = attend(info, packed, pieces)
    result = lax.all_to_all(result, "tp", 0, 0, tiled=True)

    def join(value):
        value = value.reshape(kvh, -1, group, width).transpose(1, 0, 2, 3)
        return value.reshape(-1, heads, width)

    return join(result[:, : span * group]), join(result[:, span * group :])


def solution(mesh):
    sizes = (8, 4, 2, 8)
    names = ("y", "x", "core", "tp")
    grid = Mesh(mesh.devices.reshape(sizes), names)
    rows = P(names, None, None)
    along = P(names[:3])
    return jax.shard_map(
        functools.partial(shards, sizes),
        mesh=grid,
        in_specs=(rows,) * 6 + (along, along),
        out_specs=(rows, rows),
        check_vma=False,
    )
```

```python
import functools
import math

import jax
import jax.numpy as jnp
from jax import lax
from jax.experimental import pallas as pl
from jax.experimental.pallas import tpu as pltpu
from jax.sharding import Mesh
from jax.sharding import PartitionSpec as P

BIG = -1e30
LIMIT = 2.0**100
SCALE = 128**-0.5 * math.log2(math.e)


def attend(info, packed, pieces, chunk=2048, block=768, ahead=1, near_ahead=9):
    sources = packed.shape[0]
    asked, tokens, rest_of, width, near = 288, 256, 32, 128, 512
    rows = sources * asked
    blocks = rows // block
    beacons = len(pieces) * 8 * 64
    per = chunk // 64
    slow = 512

    def scores(k, q):
        return lax.dot_general(k, q, (((1,), (1,)), ((), ())), preferred_element_type=jnp.float32)

    def kernel(info_ref, packed_ref, *rest):
        piece_refs, out_ref = rest[: len(pieces)], rest[len(pieces)]
        q2, local, far, top, total, extra = rest[len(pieces) + 1 :]
        me, own_y, reach = info_ref[0], info_ref[1], info_ref[2]
        for s in range(sources):
            at = pl.ds(s * 64, 64)
            local[at, :width] = packed_ref[s, 288:352, :]
            local[at, width:] = packed_ref[s, 352:416, :]
            scaled = packed_ref[s, 0:asked, :].astype(jnp.float32) * SCALE
            high = scaled.astype(jnp.bfloat16)
            both = jnp.concatenate([high, (scaled - high.astype(jnp.float32)).astype(jnp.bfloat16)], -1)
            q2[pl.ds(s * tokens, tokens), :] = both[:tokens]
            q2[pl.ds(sources * tokens + s * rest_of, rest_of), :] = both[tokens:]
        local[pl.ds(near, 64), :] = piece_refs[0][own_y]
        local[pl.ds(near + 64, 64), :] = jnp.zeros((64, 2 * width), jnp.bfloat16)
        count = jnp.int32(0)
        for p in range(len(pieces)):
            for y in range(8):
                owner = y * 8 + info_ref[3 + p]
                seen = (owner < me) & (owner >= me - reach)
                slot = jnp.where(seen, count, 63 - (p * 8 + y - count))
                far[pl.ds(pl.multiple_of(slot * 64, 64), 64), :] = piece_refs[p][y]
                count = count + seen.astype(jnp.int32)

        def double(kv):
            return jnp.concatenate([kv[:, :width], kv[:, :width]], -1)

        def turned(kv):
            v = kv[:, width:]
            return jnp.concatenate([v.T, jnp.ones((16, v.shape[0]), jnp.bfloat16)], 0)

        def query(r):
            return q2[pl.ds(pl.multiple_of(r * block, block), block), :]

        beacon_kv = local[near : near + 128, :]
        beacon_k = double(beacon_kv)
        local_k = double(local[:near, :])
        local_v = turned(local[:near, :])
        beacon_v = turned(beacon_kv)
        def masked(k, q, until):
            st = scores(k, q)
            return jnp.where(lax.broadcasted_iota(jnp.int32, st.shape, 0) < until, st, BIG)

        def weighed(v, st, m):
            return jnp.dot(v, jnp.exp2(st - m).astype(jnp.bfloat16), preferred_element_type=jnp.float32)

        def begin(s):
            q = q2[pl.ds(s * tokens, tokens), :]
            lane = lax.broadcasted_iota(jnp.int32, (1, tokens), 1)
            if s < sources:
                wide = -(-(s + 1) * 64 // 128) * 128
                return [(local_v[:, :wide], masked(local_k[:wide], q, s * 64 + lane // 4 + 1))]
            return [
                (local_v, masked(local_k, q, (lane // 4 + 1) * 8)),
                (beacon_v, masked(beacon_k, q, lane // 4 + 1)),
            ]

        def close(s, pairs):
            m = functools.reduce(jnp.maximum, [jnp.max(st, 0, keepdims=True) for _, st in pairs])
            block_of, lanes = s * tokens // block, pl.ds(s * tokens % block, tokens)
            top[block_of, :, lanes] = m
            total[block_of, :, lanes] = sum(weighed(v, st, m) for v, st in pairs)

        begun = []
        for s in range(sources + 1):
            begun.append((s, begin(s)))
            if len(begun) > near_ahead:
                close(*begun.pop(0))
        for item in begun:
            close(*item)

        extra[...] = jnp.zeros_like(extra)
        full = count // per
        left = count - full * per

        def sweep(start, keys):
            kv = far[pl.ds(pl.multiple_of(start, 64), chunk), :]
            k, v = double(kv), turned(kv)
            if keys is not None:
                v = jnp.where(lax.broadcasted_iota(jnp.int32, v.shape, 1) < keys, v, jnp.zeros_like(v))
            waiting = []

            def finish(r, st):
                w = jnp.exp2(st - top[r]).astype(jnp.bfloat16)
                extra[r] += jnp.dot(v, w, preferred_element_type=jnp.float32)

            for r in range(blocks):
                waiting.append((r, scores(k, query(r))))
                if len(waiting) > ahead:
                    finish(*waiting.pop(0))
            for item in waiting:
                finish(*item)

        def step(i, _):
            sweep(i * chunk, None)
            return 0

        lax.fori_loop(0, full, step, 0)

        @pl.when(left > 0)
        def _():
            sweep(full * chunk, left * 64)

        worst = jnp.max(jnp.where(extra[:, width : width + 8, :] <= LIMIT, 0.0, 1.0))

        @pl.when(worst > 0.0)
        def _():
            extra[...] = jnp.zeros_like(extra)

            def redo(i, _):
                start = pl.multiple_of(i * slow, 64)
                kv = far[pl.ds(start, slow), :]
                k, v = double(kv), turned(kv)
                inside = lax.broadcasted_iota(jnp.int32, (slow, block), 0) < count * 64 - start

                def one(r, _):
                    st = jnp.where(inside, scores(k, query(r)), BIG)
                    old = top[r]
                    m = jnp.maximum(old, jnp.max(st, 0, keepdims=True))
                    w = jnp.exp2(st - m).astype(jnp.bfloat16)
                    top[r] = m
                    total[r] = total[r] * jnp.exp2(old - m) + jnp.dot(v, w, preferred_element_type=jnp.float32)
                    return 0

                lax.fori_loop(0, blocks, one, 0)
                return 0

            lax.fori_loop(0, (count + slow // 64 - 1) // (slow // 64), redo, 0)

        parts = []
        for r in range(blocks):
            a = total[r] + extra[r]
            parts.append((a[:width] / a[width : width + 1]).T.astype(jnp.bfloat16))
        joined = jnp.concatenate(parts, 0)
        for s in range(sources):
            out_ref[s, :tokens, :] = joined[s * tokens : (s + 1) * tokens]
            behind = sources * tokens + s * rest_of
            out_ref[s, tokens:, :] = joined[behind : behind + rest_of]

    vmem = pl.BlockSpec(memory_space=pltpu.VMEM)
    return pl.pallas_call(
        kernel,
        out_shape=jax.ShapeDtypeStruct((sources, asked, width), jnp.bfloat16),
        in_specs=[pl.BlockSpec(memory_space=pltpu.SMEM)] + [vmem] * (1 + len(pieces)),
        out_specs=vmem,
        scratch_shapes=[
            pltpu.VMEM((rows, 2 * width), jnp.bfloat16),
            pltpu.VMEM((near + 128, 2 * width), jnp.bfloat16),
            pltpu.VMEM((beacons, 2 * width), jnp.bfloat16),
            pltpu.VMEM((blocks, 1, block), jnp.float32),
            pltpu.VMEM((blocks, width + 16, block), jnp.float32),
            pltpu.VMEM((blocks, width + 16, block), jnp.float32),
        ],
        compiler_params=pltpu.CompilerParams(vmem_limit_bytes=48 * 1024 * 1024),
        name="attend",
    )(info, packed, *pieces)


def memory_rows(t, places, bk, bv, copies):
    count, kvh, width = bk.shape
    half = width // 2

    def kernel(t_ref, places_ref, bk_ref, bv_ref, out_ref):
        row = lax.broadcasted_iota(jnp.int32, (count, width), 0)
        place = jnp.zeros((count, width), jnp.int32)
        for j in range(count):
            place = jnp.where(row == j, places_ref[t_ref[0] * count + j], place)
        steps = (lax.broadcasted_iota(jnp.int32, (count, width), 1) % half).astype(jnp.float32)
        angles = place.astype(jnp.float32) * jnp.exp(steps * (-2.0 * math.log(ROPE_BASE) / width))
        cosine, sine = jnp.cos(angles), jnp.sin(angles)
        sine = jnp.where(lax.broadcasted_iota(jnp.int32, (count, width), 1) < half, -sine, sine)
        wide = bk_ref[...].astype(jnp.float32)
        keys, vals = [], bv_ref[...].astype(jnp.float32)
        for h in range(kvh):
            k = wide[:, h, :]
            k = k * cosine + pltpu.roll(k, half, 1) * sine
            both = jnp.concatenate([k, vals[:, h, :]], -1).astype(jnp.bfloat16)
            for y in range(copies):
                out_ref[y * kvh + h] = both

    vmem = pl.BlockSpec(memory_space=pltpu.VMEM)
    smem = pl.BlockSpec(memory_space=pltpu.SMEM)
    return pl.pallas_call(
        kernel,
        out_shape=jax.ShapeDtypeStruct((copies * kvh, count, 2 * width), jnp.bfloat16),
        in_specs=[smem, smem, vmem, vmem],
        out_specs=vmem,
        name="memory_rows",
    )(t, places, bk, bv)


ROPE_BASE = 1000000.0


def turns(places, width):
    half = width // 2
    steps = jnp.arange(half).astype(jnp.float32)
    freqs = jnp.exp(steps * (-2.0 * math.log(ROPE_BASE) / width))
    angles = places.astype(jnp.float32)[:, None] * freqs[None, :]
    cosine, sine = jnp.cos(angles), jnp.sin(angles)
    return (
        jnp.concatenate([cosine, cosine], -1)[:, None, :],
        jnp.concatenate([-sine, sine], -1)[:, None, :],
    )


def rotate(vectors, cosine, sine):
    half = vectors.shape[-1] // 2
    wide = vectors.astype(jnp.float32)
    turned = jnp.concatenate([wide[..., half:], wide[..., :half]], -1)
    return (wide * cosine + turned * sine).astype(jnp.bfloat16)


def shift(value, axis, size, step):
    return lax.ppermute(value, axis, [(i, (i + step) % size) for i in range(size)])


def shards(sizes, queries, keys, values, bq, bk, bv, places, visible):
    ny, nx, nc, nt = sizes
    y, x, c, t = (lax.axis_index(a) for a in ("y", "x", "core", "tp"))
    me = (y * nx + x) * nc + c
    span, heads, width = queries.shape
    count = bk.shape[0]
    kvh = bk.shape[1]
    group = heads // kvh
    mine = lax.dynamic_slice_in_dim(places, t * count, count, 0)
    bturn = turns(mine, width)
    memory = memory_rows(t.reshape(1), places, bk, bv, ny)
    own = lax.all_to_all(memory, ("y", "tp"), 0, 0, tiled=True)
    own = own.reshape(ny, nt * count, 2 * width)
    steps = (1, nx - 1, 2)
    pieces = [own] + [shift(own, "x", nx, d) for d in steps]
    pieces = pieces + [shift(p, "core", nc, 1) for p in pieces]
    column = [lax.rem(x + nx - d, nx) for d in (0,) + steps]
    labels = [a * nc + c for a in column] + [a * nc + 1 - c for a in column]
    info = jnp.stack([me, y, visible[0]] + labels).astype(jnp.int32)

    turn = turns(me * span * nt + t * span + jnp.arange(span), width)

    def split(value):
        value = value.reshape(value.shape[0], kvh, -1, width).transpose(1, 0, 2, 3)
        return value.reshape(kvh, -1, width)

    packed = jnp.concatenate(
        [split(rotate(queries, *turn)), split(rotate(bq, *bturn)), split(rotate(keys, *turn)), split(values)], 1
    )
    packed, info = lax.optimization_barrier((packed, info))
    packed = lax.all_to_all(packed, "tp", 0, 0, tiled=True)
    result = attend(info, packed, pieces)
    result = lax.all_to_all(result, "tp", 0, 0, tiled=True)

    def join(value):
        value = value.reshape(kvh, -1, group, width).transpose(1, 0, 2, 3)
        return value.reshape(-1, heads, width)

    return join(result[:, : span * group]), join(result[:, span * group :])


def solution(mesh):
    sizes = (8, 4, 2, 8)
    names = ("y", "x", "core", "tp")
    grid = Mesh(mesh.devices.reshape(sizes), names)
    rows = P(names, None, None)
    along = P(names[:3])
    return jax.shard_map(
        functools.partial(shards, sizes),
        mesh=grid,
        in_specs=(rows,) * 6 + (along, along),
        out_specs=(rows, rows),
        check_vma=False,
    )
```

```python
import functools
import math

import jax
import jax.numpy as jnp
from jax import lax
from jax.experimental import pallas as pl
from jax.experimental.pallas import tpu as pltpu
from jax.sharding import Mesh
from jax.sharding import PartitionSpec as P

BIG = -1e30
LIMIT = 2.0**100
SCALE = 128**-0.5 * math.log2(math.e)


def attend(info, packed, pieces, chunk=2048, block=768, ahead=1, near_ahead=9):
    sources = packed.shape[0]
    asked, tokens, rest_of, width, near = 288, 256, 32, 128, 512
    rows = sources * asked
    blocks = rows // block
    beacons = len(pieces) * 8 * 64
    per = chunk // 64
    slow = 512

    def scores(k, q):
        return lax.dot_general(k, q, (((1,), (1,)), ((), ())), preferred_element_type=jnp.float32)

    def kernel(info_ref, packed_ref, *rest):
        piece_refs, out_ref = rest[: len(pieces)], rest[len(pieces)]
        q2, local, far, top, total, extra = rest[len(pieces) + 1 :]
        me, own_y, reach = info_ref[0], info_ref[1], info_ref[2]
        for s in range(sources):
            at = pl.ds(s * 64, 64)
            local[at, :width] = packed_ref[s, 288:352, :]
            local[at, width:] = packed_ref[s, 352:416, :]
            scaled = packed_ref[s, 0:asked, :].astype(jnp.float32) * SCALE
            high = scaled.astype(jnp.bfloat16)
            both = jnp.concatenate([high, (scaled - high.astype(jnp.float32)).astype(jnp.bfloat16)], -1)
            q2[pl.ds(s * tokens, tokens), :] = both[:tokens]
            q2[pl.ds(sources * tokens + s * rest_of, rest_of), :] = both[tokens:]
        local[pl.ds(near, 64), :] = piece_refs[0][own_y]
        local[pl.ds(near + 64, 64), :] = jnp.zeros((64, 2 * width), jnp.bfloat16)
        count = jnp.int32(0)
        for p in range(len(pieces)):
            for y in range(8):
                owner = y * 8 + info_ref[3 + p]
                seen = (owner < me) & (owner >= me - reach)
                slot = jnp.where(seen, count, 63 - (p * 8 + y - count))
                far[pl.ds(pl.multiple_of(slot * 64, 64), 64), :] = piece_refs[p][y]
                count = count + seen.astype(jnp.int32)

        def double(kv):
            return jnp.concatenate([kv[:, :width], kv[:, :width]], -1)

        def turned(kv):
            v = kv[:, width:]
            return jnp.concatenate([v.T, jnp.ones((16, v.shape[0]), jnp.bfloat16)], 0)

        def query(r):
            return q2[pl.ds(pl.multiple_of(r * block, block), block), :]

        beacon_kv = local[near : near + 128, :]
        beacon_k = double(beacon_kv)
        local_k = double(local[:near, :])
        local_v = turned(local[:near, :])
        beacon_v = turned(beacon_kv)
        def masked(k, q, until):
            st = scores(k, q)
            return jnp.where(lax.broadcasted_iota(jnp.int32, st.shape, 0) < until, st, BIG)

        def weighed(v, st, m):
            return jnp.dot(v, jnp.exp2(st - m).astype(jnp.bfloat16), preferred_element_type=jnp.float32)

        def begin(s):
            q = q2[pl.ds(s * tokens, tokens), :]
            lane = lax.broadcasted_iota(jnp.int32, (1, tokens), 1)
            if s < sources:
                wide = -(-(s + 1) * 64 // 128) * 128
                return [(local_v[:, :wide], masked(local_k[:wide], q, s * 64 + lane // 4 + 1))]
            return [
                (local_v, masked(local_k, q, (lane // 4 + 1) * 8)),
                (beacon_v, masked(beacon_k, q, lane // 4 + 1)),
            ]

        def close(s, pairs):
            m = functools.reduce(jnp.maximum, [jnp.max(st, 0, keepdims=True) for _, st in pairs])
            block_of, lanes = s * tokens // block, pl.ds(s * tokens % block, tokens)
            top[block_of, :, lanes] = m
            total[block_of, :, lanes] = sum(weighed(v, st, m) for v, st in pairs)

        begun = []
        for s in range(sources + 1):
            begun.append((s, begin(s)))
            if len(begun) > near_ahead:
                close(*begun.pop(0))
        for item in begun:
            close(*item)

        extra[...] = jnp.zeros_like(extra)
        full = count // per
        left = count - full * per

        def sweep(start, keys):
            kv = far[pl.ds(pl.multiple_of(start, 64), chunk), :]
            k, v = double(kv), turned(kv)
            if keys is not None:
                v = jnp.where(lax.broadcasted_iota(jnp.int32, v.shape, 1) < keys, v, jnp.zeros_like(v))
            waiting = []

            def finish(r, st):
                w = jnp.exp2(st - top[r]).astype(jnp.bfloat16)
                extra[r] += jnp.dot(v, w, preferred_element_type=jnp.float32)

            for r in range(blocks):
                waiting.append((r, scores(k, query(r))))
                if len(waiting) > ahead:
                    finish(*waiting.pop(0))
            for item in waiting:
                finish(*item)

        def step(i, _):
            sweep(i * chunk, None)
            return 0

        lax.fori_loop(0, full, step, 0)

        @pl.when(left > 0)
        def _():
            sweep(full * chunk, left * 64)

        worst = jnp.max(jnp.where(extra[:, width : width + 8, :] <= LIMIT, 0.0, 1.0))

        @pl.when(worst > 0.0)
        def _():
            extra[...] = jnp.zeros_like(extra)

            def redo(i, _):
                start = pl.multiple_of(i * slow, 64)
                kv = far[pl.ds(start, slow), :]
                k, v = double(kv), turned(kv)
                inside = lax.broadcasted_iota(jnp.int32, (slow, block), 0) < count * 64 - start

                def one(r, _):
                    st = jnp.where(inside, scores(k, query(r)), BIG)
                    old = top[r]
                    m = jnp.maximum(old, jnp.max(st, 0, keepdims=True))
                    w = jnp.exp2(st - m).astype(jnp.bfloat16)
                    top[r] = m
                    total[r] = total[r] * jnp.exp2(old - m) + jnp.dot(v, w, preferred_element_type=jnp.float32)
                    return 0

                lax.fori_loop(0, blocks, one, 0)
                return 0

            lax.fori_loop(0, (count + slow // 64 - 1) // (slow // 64), redo, 0)

        parts = []
        for r in range(blocks):
            a = total[r] + extra[r]
            parts.append((a[:width] / a[width : width + 1]).T.astype(jnp.bfloat16))
        joined = jnp.concatenate(parts, 0)
        for s in range(sources):
            out_ref[s, :tokens, :] = joined[s * tokens : (s + 1) * tokens]
            behind = sources * tokens + s * rest_of
            out_ref[s, tokens:, :] = joined[behind : behind + rest_of]

    vmem = pl.BlockSpec(memory_space=pltpu.VMEM)
    return pl.pallas_call(
        kernel,
        out_shape=jax.ShapeDtypeStruct((sources, asked, width), jnp.bfloat16),
        in_specs=[pl.BlockSpec(memory_space=pltpu.SMEM)] + [vmem] * (1 + len(pieces)),
        out_specs=vmem,
        scratch_shapes=[
            pltpu.VMEM((rows, 2 * width), jnp.bfloat16),
            pltpu.VMEM((near + 128, 2 * width), jnp.bfloat16),
            pltpu.VMEM((beacons, 2 * width), jnp.bfloat16),
            pltpu.VMEM((blocks, 1, block), jnp.float32),
            pltpu.VMEM((blocks, width + 16, block), jnp.float32),
            pltpu.VMEM((blocks, width + 16, block), jnp.float32),
        ],
        compiler_params=pltpu.CompilerParams(vmem_limit_bytes=48 * 1024 * 1024),
        name="attend",
    )(info, packed, *pieces)


def memory_rows(t, places, bk, bv, copies):
    count, kvh, width = bk.shape
    half = width // 2

    def kernel(t_ref, places_ref, bk_ref, bv_ref, out_ref):
        row = lax.broadcasted_iota(jnp.int32, (count, width), 0)
        place = jnp.zeros((count, width), jnp.int32)
        for j in range(count):
            place = jnp.where(row == j, places_ref[t_ref[0] * count + j], place)
        steps = (lax.broadcasted_iota(jnp.int32, (count, width), 1) % half).astype(jnp.float32)
        angles = place.astype(jnp.float32) * jnp.exp(steps * (-2.0 * math.log(ROPE_BASE) / width))
        cosine, sine = jnp.cos(angles), jnp.sin(angles)
        sine = jnp.where(lax.broadcasted_iota(jnp.int32, (count, width), 1) < half, -sine, sine)
        wide = bk_ref[...].astype(jnp.float32)
        keys, vals = [], bv_ref[...].astype(jnp.float32)
        for h in range(kvh):
            k = wide[:, h, :]
            k = k * cosine + pltpu.roll(k, half, 1) * sine
            both = jnp.concatenate([k, vals[:, h, :]], -1).astype(jnp.bfloat16)
            for y in range(copies):
                out_ref[y * kvh + h] = both

    vmem = pl.BlockSpec(memory_space=pltpu.VMEM)
    smem = pl.BlockSpec(memory_space=pltpu.SMEM)
    return pl.pallas_call(
        kernel,
        out_shape=jax.ShapeDtypeStruct((copies * kvh, count, 2 * width), jnp.bfloat16),
        in_specs=[smem, smem, vmem, vmem],
        out_specs=vmem,
        name="memory_rows",
    )(t, places, bk, bv)


ROPE_BASE = 1000000.0


def turns(places, width):
    half = width // 2
    steps = jnp.arange(half).astype(jnp.float32)
    freqs = jnp.exp(steps * (-2.0 * math.log(ROPE_BASE) / width))
    angles = places.astype(jnp.float32)[:, None] * freqs[None, :]
    cosine, sine = jnp.cos(angles), jnp.sin(angles)
    return (
        jnp.concatenate([cosine, cosine], -1)[:, None, :],
        jnp.concatenate([-sine, sine], -1)[:, None, :],
    )


def rotate(vectors, cosine, sine):
    half = vectors.shape[-1] // 2
    wide = vectors.astype(jnp.float32)
    turned = jnp.concatenate([wide[..., half:], wide[..., :half]], -1)
    return (wide * cosine + turned * sine).astype(jnp.bfloat16)


def shift(value, axis, size, step):
    return lax.ppermute(value, axis, [(i, (i + step) % size) for i in range(size)])


def shards(sizes, queries, keys, values, bq, bk, bv, places, visible):
    ny, nx, nc, nt = sizes
    y, x, c, t = (lax.axis_index(a) for a in ("y", "x", "core", "tp"))
    me = (y * nx + x) * nc + c
    span, heads, width = queries.shape
    count = bk.shape[0]
    kvh = bk.shape[1]
    group = heads // kvh
    mine = lax.dynamic_slice_in_dim(places, t * count, count, 0)
    bturn = turns(mine, width)
    memory = memory_rows(t.reshape(1), places, bk, bv, ny)
    own = lax.all_to_all(memory, ("y", "tp"), 0, 0, tiled=True)
    own = own.reshape(ny, nt * count, 2 * width)
    steps = (2, 1, nx - 1)
    pieces = [own] + [shift(own, "x", nx, d) for d in steps]
    pieces = pieces + [shift(p, "core", nc, 1) for p in pieces]
    column = [lax.rem(x + nx - d, nx) for d in (0,) + steps]
    labels = [a * nc + c for a in column] + [a * nc + 1 - c for a in column]
    info = jnp.stack([me, y, visible[0]] + labels).astype(jnp.int32)

    turn = turns(me * span * nt + t * span + jnp.arange(span), width)

    def split(value):
        value = value.reshape(value.shape[0], kvh, -1, width).transpose(1, 0, 2, 3)
        return value.reshape(kvh, -1, width)

    packed = jnp.concatenate(
        [split(rotate(queries, *turn)), split(rotate(bq, *bturn)), split(rotate(keys, *turn)), split(values)], 1
    )
    packed, info = lax.optimization_barrier((packed, info))
    packed = lax.all_to_all(packed, "tp", 0, 0, tiled=True)
    result = attend(info, packed, pieces)
    result = lax.all_to_all(result, "tp", 0, 0, tiled=True)

    def join(value):
        value = value.reshape(kvh, -1, group, width).transpose(1, 0, 2, 3)
        return value.reshape(-1, heads, width)

    return join(result[:, : span * group]), join(result[:, span * group :])


def solution(mesh):
    sizes = (8, 4, 2, 8)
    names = ("y", "x", "core", "tp")
    grid = Mesh(mesh.devices.reshape(sizes), names)
    rows = P(names, None, None)
    along = P(names[:3])
    return jax.shard_map(
        functools.partial(shards, sizes),
        mesh=grid,
        in_specs=(rows,) * 6 + (along, along),
        out_specs=(rows, rows),
        check_vma=False,
    )
```

```python
import functools
import math

import jax
import jax.numpy as jnp
from jax import lax
from jax.experimental import pallas as pl
from jax.experimental.pallas import tpu as pltpu
from jax.sharding import Mesh
from jax.sharding import PartitionSpec as P

BIG = -1e30
LIMIT = 2.0**100
SCALE = 128**-0.5 * math.log2(math.e)


def attend(info, packed, pieces, chunk=2048, block=768, ahead=1, near_ahead=9):
    sources = packed.shape[0]
    asked, tokens, rest_of, width, near = 288, 256, 32, 128, 512
    rows = sources * asked
    blocks = rows // block
    beacons = len(pieces) * 8 * 64
    per = chunk // 64
    slow = 512

    def scores(k, q):
        return lax.dot_general(k, q, (((1,), (1,)), ((), ())), preferred_element_type=jnp.float32)

    def kernel(info_ref, packed_ref, *rest):
        piece_refs, out_ref = rest[: len(pieces)], rest[len(pieces)]
        q2, local, far, top, total, extra = rest[len(pieces) + 1 :]
        me, own_y, reach = info_ref[0], info_ref[1], info_ref[2]
        for s in range(sources):
            at = pl.ds(s * 64, 64)
            local[at, :width] = packed_ref[s, 288:352, :]
            local[at, width:] = packed_ref[s, 352:416, :]
            scaled = packed_ref[s, 0:asked, :].astype(jnp.float32) * SCALE
            high = scaled.astype(jnp.bfloat16)
            both = jnp.concatenate([high, (scaled - high.astype(jnp.float32)).astype(jnp.bfloat16)], -1)
            q2[pl.ds(s * tokens, tokens), :] = both[:tokens]
            q2[pl.ds(sources * tokens + s * rest_of, rest_of), :] = both[tokens:]
        local[pl.ds(near, 64), :] = piece_refs[0][own_y]
        local[pl.ds(near + 64, 64), :] = jnp.zeros((64, 2 * width), jnp.bfloat16)
        count = jnp.int32(0)
        for p in range(len(pieces)):
            for y in range(8):
                owner = y * 8 + info_ref[3 + p]
                seen = (owner < me) & (owner >= me - reach)
                slot = jnp.where(seen, count, 63 - (p * 8 + y - count))
                far[pl.ds(pl.multiple_of(slot * 64, 64), 64), :] = piece_refs[p][y]
                count = count + seen.astype(jnp.int32)

        def double(kv):
            return jnp.concatenate([kv[:, :width], kv[:, :width]], -1)

        def turned(kv):
            v = kv[:, width:]
            return jnp.concatenate([v.T, jnp.ones((16, v.shape[0]), jnp.bfloat16)], 0)

        def query(r):
            return q2[pl.ds(pl.multiple_of(r * block, block), block), :]

        beacon_kv = local[near : near + 128, :]
        beacon_k = double(beacon_kv)
        local_k = double(local[:near, :])
        local_v = turned(local[:near, :])
        beacon_v = turned(beacon_kv)
        def masked(k, q, until):
            st = scores(k, q)
            return jnp.where(lax.broadcasted_iota(jnp.int32, st.shape, 0) < until, st, BIG)

        def weighed(v, st, m):
            return jnp.dot(v, jnp.exp2(st - m).astype(jnp.bfloat16), preferred_element_type=jnp.float32)

        def begin(s):
            q = q2[pl.ds(s * tokens, tokens), :]
            lane = lax.broadcasted_iota(jnp.int32, (1, tokens), 1)
            if s < sources:
                wide = -(-(s + 1) * 64 // 128) * 128
                return [(local_v[:, :wide], masked(local_k[:wide], q, s * 64 + lane // 4 + 1))]
            return [
                (local_v, masked(local_k, q, (lane // 4 + 1) * 8)),
                (beacon_v, masked(beacon_k, q, lane // 4 + 1)),
            ]

        def close(s, pairs):
            m = functools.reduce(jnp.maximum, [jnp.max(st, 0, keepdims=True) for _, st in pairs])
            block_of, lanes = s * tokens // block, pl.ds(s * tokens % block, tokens)
            top[block_of, :, lanes] = m
            total[block_of, :, lanes] = sum(weighed(v, st, m) for v, st in pairs)

        begun = []
        for s in range(sources + 1):
            begun.append((s, begin(s)))
            if len(begun) > near_ahead:
                close(*begun.pop(0))
        for item in begun:
            close(*item)

        extra[...] = jnp.zeros_like(extra)
        full = count // per
        left = count - full * per

        def sweep(start, keys):
            kv = far[pl.ds(pl.multiple_of(start, 64), chunk), :]
            k, v = double(kv), turned(kv)
            if keys is not None:
                v = jnp.where(lax.broadcasted_iota(jnp.int32, v.shape, 1) < keys, v, jnp.zeros_like(v))
            waiting = []

            def finish(r, st):
                w = jnp.exp2(st - top[r]).astype(jnp.bfloat16)
                extra[r] += jnp.dot(v, w, preferred_element_type=jnp.float32)

            for r in range(blocks):
                waiting.append((r, scores(k, query(r))))
                if len(waiting) > ahead:
                    finish(*waiting.pop(0))
            for item in waiting:
                finish(*item)

        def step(i, _):
            sweep(i * chunk, None)
            return 0

        lax.fori_loop(0, full, step, 0)

        @pl.when(left > 0)
        def _():
            sweep(full * chunk, left * 64)

        worst = jnp.max(jnp.where(extra[:, width : width + 8, :] <= LIMIT, 0.0, 1.0))

        @pl.when(worst > 0.0)
        def _():
            extra[...] = jnp.zeros_like(extra)

            def redo(i, _):
                start = pl.multiple_of(i * slow, 64)
                kv = far[pl.ds(start, slow), :]
                k, v = double(kv), turned(kv)
                inside = lax.broadcasted_iota(jnp.int32, (slow, block), 0) < count * 64 - start

                def one(r, _):
                    st = jnp.where(inside, scores(k, query(r)), BIG)
                    old = top[r]
                    m = jnp.maximum(old, jnp.max(st, 0, keepdims=True))
                    w = jnp.exp2(st - m).astype(jnp.bfloat16)
                    top[r] = m
                    total[r] = total[r] * jnp.exp2(old - m) + jnp.dot(v, w, preferred_element_type=jnp.float32)
                    return 0

                lax.fori_loop(0, blocks, one, 0)
                return 0

            lax.fori_loop(0, (count + slow // 64 - 1) // (slow // 64), redo, 0)

        parts = []
        for r in range(blocks):
            a = total[r] + extra[r]
            parts.append((a[:width] / a[width : width + 1]).T.astype(jnp.bfloat16))
        joined = jnp.concatenate(parts, 0)
        for s in range(sources):
            out_ref[s, :tokens, :] = joined[s * tokens : (s + 1) * tokens]
            behind = sources * tokens + s * rest_of
            out_ref[s, tokens:, :] = joined[behind : behind + rest_of]

    vmem = pl.BlockSpec(memory_space=pltpu.VMEM)
    return pl.pallas_call(
        kernel,
        out_shape=jax.ShapeDtypeStruct((sources, asked, width), jnp.bfloat16),
        in_specs=[pl.BlockSpec(memory_space=pltpu.SMEM)] + [vmem] * (1 + len(pieces)),
        out_specs=vmem,
        scratch_shapes=[
            pltpu.VMEM((rows, 2 * width), jnp.bfloat16),
            pltpu.VMEM((near + 128, 2 * width), jnp.bfloat16),
            pltpu.VMEM((beacons, 2 * width), jnp.bfloat16),
            pltpu.VMEM((blocks, 1, block), jnp.float32),
            pltpu.VMEM((blocks, width + 16, block), jnp.float32),
            pltpu.VMEM((blocks, width + 16, block), jnp.float32),
        ],
        compiler_params=pltpu.CompilerParams(vmem_limit_bytes=48 * 1024 * 1024),
        name="attend",
    )(info, packed, *pieces)


def memory_rows(t, places, bk, bv, copies):
    count, kvh, width = bk.shape
    half = width // 2

    def kernel(t_ref, places_ref, bk_ref, bv_ref, out_ref):
        row = lax.broadcasted_iota(jnp.int32, (count, width), 0)
        place = jnp.zeros((count, width), jnp.int32)
        for j in range(count):
            place = jnp.where(row == j, places_ref[t_ref[0] * count + j], place)
        steps = (lax.broadcasted_iota(jnp.int32, (count, width), 1) % half).astype(jnp.float32)
        angles = place.astype(jnp.float32) * jnp.exp(steps * (-2.0 * math.log(ROPE_BASE) / width))
        cosine, sine = jnp.cos(angles), jnp.sin(angles)
        sine = jnp.where(lax.broadcasted_iota(jnp.int32, (count, width), 1) < half, -sine, sine)
        wide = bk_ref[...].astype(jnp.float32)
        keys, vals = [], bv_ref[...].astype(jnp.float32)
        for h in range(kvh):
            k = wide[:, h, :]
            k = k * cosine + pltpu.roll(k, half, 1) * sine
            both = jnp.concatenate([k, vals[:, h, :]], -1).astype(jnp.bfloat16)
            for y in range(copies):
                out_ref[y * kvh + h] = both

    vmem = pl.BlockSpec(memory_space=pltpu.VMEM)
    smem = pl.BlockSpec(memory_space=pltpu.SMEM)
    return pl.pallas_call(
        kernel,
        out_shape=jax.ShapeDtypeStruct((copies * kvh, count, 2 * width), jnp.bfloat16),
        in_specs=[smem, smem, vmem, vmem],
        out_specs=vmem,
        name="memory_rows",
    )(t, places, bk, bv)


ROPE_BASE = 1000000.0


def turns(places, width):
    half = width // 2
    steps = jnp.arange(half).astype(jnp.float32)
    freqs = jnp.exp(steps * (-2.0 * math.log(ROPE_BASE) / width))
    angles = places.astype(jnp.float32)[:, None] * freqs[None, :]
    cosine, sine = jnp.cos(angles), jnp.sin(angles)
    return (
        jnp.concatenate([cosine, cosine], -1)[:, None, :],
        jnp.concatenate([-sine, sine], -1)[:, None, :],
    )


def rotate(vectors, cosine, sine):
    half = vectors.shape[-1] // 2
    wide = vectors.astype(jnp.float32)
    turned = jnp.concatenate([wide[..., half:], wide[..., :half]], -1)
    return (wide * cosine + turned * sine).astype(jnp.bfloat16)


def shift(value, axis, size, step):
    return lax.ppermute(value, axis, [(i, (i + step) % size) for i in range(size)])


def shards(sizes, queries, keys, values, bq, bk, bv, places, visible):
    ny, nx, nc, nt = sizes
    y, x, c, t = (lax.axis_index(a) for a in ("y", "x", "core", "tp"))
    me = (y * nx + x) * nc + c
    span, heads, width = queries.shape
    count = bk.shape[0]
    kvh = bk.shape[1]
    group = heads // kvh
    mine = lax.dynamic_slice_in_dim(places, t * count, count, 0)
    bturn = turns(mine, width)
    memory = memory_rows(t.reshape(1), places, bk, bv, ny)
    own = lax.all_to_all(memory, ("y", "tp"), 0, 0, tiled=True)
    own = own.reshape(ny, nt * count, 2 * width)
    steps = (2, nx - 1, 1)
    pieces = [own] + [shift(own, "x", nx, d) for d in steps]
    pieces = pieces + [shift(p, "core", nc, 1) for p in pieces]
    column = [lax.rem(x + nx - d, nx) for d in (0,) + steps]
    labels = [a * nc + c for a in column] + [a * nc + 1 - c for a in column]
    info = jnp.stack([me, y, visible[0]] + labels).astype(jnp.int32)

    turn = turns(me * span * nt + t * span + jnp.arange(span), width)

    def split(value):
        value = value.reshape(value.shape[0], kvh, -1, width).transpose(1, 0, 2, 3)
        return value.reshape(kvh, -1, width)

    packed = jnp.concatenate(
        [split(rotate(queries, *turn)), split(rotate(bq, *bturn)), split(rotate(keys, *turn)), split(values)], 1
    )
    packed, info = lax.optimization_barrier((packed, info))
    packed = lax.all_to_all(packed, "tp", 0, 0, tiled=True)
    result = attend(info, packed, pieces)
    result = lax.all_to_all(result, "tp", 0, 0, tiled=True)

    def join(value):
        value = value.reshape(kvh, -1, group, width).transpose(1, 0, 2, 3)
        return value.reshape(-1, heads, width)

    return join(result[:, : span * group]), join(result[:, span * group :])


def solution(mesh):
    sizes = (8, 4, 2, 8)
    names = ("y", "x", "core", "tp")
    grid = Mesh(mesh.devices.reshape(sizes), names)
    rows = P(names, None, None)
    along = P(names[:3])
    return jax.shard_map(
        functools.partial(shards, sizes),
        mesh=grid,
        in_specs=(rows,) * 6 + (along, along),
        out_specs=(rows, rows),
        check_vma=False,
    )
```
